32 devices in a mesh: ctx: 8 (over y, x, core), head: 4 (over z).
Axes of the slice: x: 2, y: 2, z: 4, core: 2. Of those that a mesh axis runs over, the one named last changes fastest.
Arguments:
- query_rows: bfloat16 [4096, 2048], P('ctx', 'head'), may hold values from -245 to 245
- key_rows: bfloat16 [4096, 2048], P('ctx', 'head'), may hold values from -20.5 to 20.5
- value_rows: bfloat16 [4096, 2048], P('ctx', 'head'), may hold values from -6 to 6
- segment_ids: int32 [4096], replicated, may hold values from 0 to 63, never falling along the last dimension, each value on 1 to 256 neighbouring positions
- out_weight: bfloat16 [2048, 2048], P('head'), may hold values from -0.375 to 0.375
- emg_signal: bfloat16 [64, 4096], P(None, 'ctx'), may hold values from -6 to 6
- stencil_taps: bfloat16 [5, 64, 4096], P(None, None, 'ctx'), may hold values from -4 to 4
- emg_weight: bfloat16 [64, 2048], replicated, may hold values from -0.75 to 0.75
- out_grad: bfloat16 [4096, 2048], P('ctx', 'head'), may hold values from -6 to 6
Outputs:
- layer_out: bfloat16 [4096, 2048], P('ctx', 'head')
- grad_queries: bfloat16 [4096, 2048], P('ctx', 'head')
- grad_keys: bfloat16 [4096, 2048], P('ctx', 'head')
- grad_values: bfloat16 [4096, 2048], P('ctx', 'head')
- grad_emg: bfloat16 [64, 4096], P(None, 'ctx')
The draws below stay inside these ranges and needn't reach their ends.
Inputs may be any that keep to these rules, and one draw needn't show every extreme that they name: `segment_ids`: segment ids never fall along the sequence, and every id from 0 to the largest occurs.
All inputs are finite; a program needn't handle non-finite values.
Results may differ from the reference program's by a relative error of at most 0.03.
Values may be sent and summed in bfloat16 or wider, within the bound.
A program may use at most 128 MiB of HBM per device.

```python
import math
import jax
import jax.numpy as jnp
import numpy as np
from jax import lax

D = 2048
H = 16
DH = 128
CHANNELS = 64
REACH = 2
TOK_DEV = 512
TAPS = 5
TOKENS = 4096


def paired_rows(key):
    base_key = jax.random.fold_in(key, 71)
    query_key, key_key = jax.random.split(base_key, 2)
    spread = 1.7
    key_rows = jnp.clip(jax.random.normal(key_key, (TOKENS, H * DH), jnp.float32), -6.0, 6.0) * spread
    query_rows = jnp.clip(jax.random.normal(query_key, (TOKENS, H * DH), jnp.float32), -6.0, 6.0) * spread
    return (query_rows, key_rows)


def draw_query_rows(key, part):
    return paired_rows(key)[0].astype(jnp.bfloat16)


def draw_key_rows(key, part):
    return paired_rows(key)[1].astype(jnp.bfloat16)


def block_levels(rng, dims, pieces, low, high):
    factor_of = 1.0
    for dim, blocks in pieces:
        draws = jax.random.uniform(jax.random.fold_in(jax.random.fold_in(rng, 6), dim), (blocks,), jnp.float32, low / len(pieces), high / len(pieces))
        factor_of = factor_of * jnp.repeat(jnp.exp(draws), dims[dim] // blocks).reshape((-1,) + (1,) * (len(dims) - 1 - dim))
    return factor_of


def length_profile(count, total, bound, lean):
    loads = [(1 << 20) // math.isqrt(standing ** lean) + 1 for standing in range(2, count + 1)]
    spare, holding = total - bound - (count - 1), [1] * (count - 1)
    while spare > 0:
        candidates = [i for i in range(count - 1) if holding[i] < bound]
        whole, budget = sum([loads[i] for i in candidates]), spare
        for i in candidates:
            extra = min(bound - holding[i], max(1, budget * loads[i] // whole), spare)
            holding[i] = holding[i] + extra
            spare = spare - extra
    return np.array([bound] + holding)


def uneven_parts(stream_key, amount, total, most, lean):
    if amount == 2:
        one = jax.random.randint(stream_key, (), max(1, total - most), min(most, total - 1) + 1)
        return jnp.stack([one, total - one])
    sizes = jnp.asarray(length_profile(amount, total, most, lean), jnp.int32)
    twos = (amount - 1) // 2
    source_of, taker = sizes[1:1 + 2 * twos:2], sizes[2:2 + 2 * twos:2]
    slack = jnp.minimum(source_of - 1, most - taker)
    shifted = jax.random.randint(jax.random.fold_in(stream_key, 1), (twos,), 0, 1 << 20) % (slack + 1)
    sizes = sizes.at[1:1 + 2 * twos:2].set(source_of - shifted).at[2:2 + 2 * twos:2].set(taker + shifted)
    return sizes[jax.random.permutation(jax.random.fold_in(stream_key, 2), amount)]


def bell_draw(rng, extent, scale, bound, pieces=(), dtype=jnp.bfloat16):
    entries = jax.random.normal(rng, extent, jnp.float32) * scale
    if len(pieces) > 0:
        entries = block_levels(rng, extent, pieces, -0.22, 0.18) * entries
    return jnp.clip(entries, min=-bound, max=bound).astype(dtype)


def setup_inputs(seed: int = 0) -> dict:
    seeds = jax.random.split(jax.random.key(seed), 10)
    query_rows = draw_query_rows(jax.random.fold_in(seeds[9], 71), 0)
    key_rows = draw_key_rows(jax.random.fold_in(seeds[9], 71), 0)
    value_rows = bell_draw(seeds[2], (TOKENS, H * DH), 1.0, 6.0, ((0, 8), (1, 4)))
    segment_ids = jnp.searchsorted(jnp.cumsum(uneven_parts(seeds[3], max(4, TOKENS // 64), TOKENS, min(256, TOKENS // 2), 2)), jnp.arange(TOKENS), side="right").astype(jnp.int32)
    out_weight = bell_draw(seeds[4], (H * DH, D), (H * DH // 8) ** -0.5, 0.375, ((0, 4),))
    emg_signal = bell_draw(seeds[5], (CHANNELS, TOKENS), 1.0, 6.0, ((1, 8),))
    stencil_taps = bell_draw(seeds[6], (TAPS, CHANNELS, TOKENS), 0.5, 4.0, ((2, 8),))
    emg_weight = bell_draw(seeds[7], (CHANNELS, D), CHANNELS ** -0.5, 0.75)
    out_grad = bell_draw(seeds[8], (TOKENS, D), 1.0, 6.0, ((0, 8), (1, 4)))
    return dict(query_rows=query_rows, key_rows=key_rows, value_rows=value_rows, segment_ids=segment_ids, out_weight=out_weight, emg_signal=emg_signal, stencil_taps=stencil_taps, emg_weight=emg_weight, out_grad=out_grad)


MASKED = -1.0e30


def split_heads(matrix):
    return matrix.reshape(TOKENS, H, DH).transpose(1, 0, 2)


def join_heads(stacked):
    return stacked.transpose(1, 0, 2).reshape(TOKENS, H * DH)


def forward_head(query_head, key_head, value_head, segment_ids):
    score_scale = DH ** -0.5
    query_blocks = query_head.reshape(TOKENS // TOK_DEV, TOK_DEV, DH)
    segment_blocks = segment_ids.reshape(TOKENS // TOK_DEV, TOK_DEV)

    def one_block(state_in, block_pair):
        query_block, query_segs = block_pair
        scores = jnp.dot(query_block, key_head.T, preferred_element_type=jnp.float32) * score_scale
        allowed = segment_ids[None, :] <= query_segs[:, None]
        scores = jnp.where(allowed, scores, MASKED)
        row_top = jnp.max(scores, axis=1)
        weights = jnp.where(allowed, jnp.exp(scores - row_top[:, None]), 0.0)
        row_total = jnp.sum(weights, axis=1)
        mixed = jnp.dot(weights.astype(jnp.bfloat16), value_head, preferred_element_type=jnp.float32)
        attended = (mixed / row_total[:, None]).astype(jnp.bfloat16)
        return state_in, (attended, row_top + jnp.log(row_total))

    unused, outputs = lax.scan(one_block, jnp.zeros((), jnp.float32), (query_blocks, segment_blocks))
    return outputs[0].reshape(TOKENS, DH), outputs[1].reshape(TOKENS)


def backward_head(query_head, key_head, value_head, grad_head, log_total, row_delta, segment_ids):
    score_scale = DH ** -0.5
    blocks = TOKENS // TOK_DEV
    inputs = (query_head.reshape(blocks, TOK_DEV, DH), grad_head.reshape(blocks, TOK_DEV, DH),
              log_total.reshape(blocks, TOK_DEV), row_delta.reshape(blocks, TOK_DEV),
              segment_ids.reshape(blocks, TOK_DEV))

    def one_block(state_in, block_set):
        key_grad, value_grad = state_in
        query_block, grad_block, total_block, delta_block, query_segs = block_set
        scores = jnp.dot(query_block, key_head.T, preferred_element_type=jnp.float32) * score_scale
        allowed = segment_ids[None, :] <= query_segs[:, None]
        scores = jnp.where(allowed, scores, MASKED)
        probs = jnp.where(allowed, jnp.exp(scores - total_block[:, None]), 0.0)
        weight_grad = jnp.dot(grad_block, value_head.T, preferred_element_type=jnp.float32)
        score_grad = (probs * (weight_grad - delta_block[:, None])).astype(jnp.bfloat16)
        value_grad = value_grad + jnp.dot(probs.astype(jnp.bfloat16).T, grad_block, preferred_element_type=jnp.float32)
        key_grad = key_grad + jnp.dot(score_grad.T, query_block, preferred_element_type=jnp.float32)
        query_grad = (jnp.dot(score_grad, key_head, preferred_element_type=jnp.float32) * score_scale).astype(jnp.bfloat16)
        return (key_grad, value_grad), query_grad

    zeros = jnp.zeros((TOKENS, DH), jnp.float32)
    sums, query_grad = lax.scan(one_block, (zeros, zeros), inputs)
    key_grad = (sums[0] * score_scale).astype(jnp.bfloat16)
    return query_grad.reshape(TOKENS, DH), key_grad, sums[1].astype(jnp.bfloat16)


def reference(query_rows, key_rows, value_rows, segment_ids, out_weight, emg_signal, stencil_taps, emg_weight, out_grad):
    query_heads = split_heads(query_rows)
    key_heads = split_heads(key_rows)
    value_heads = split_heads(value_rows)

    def forward_one(triple):
        return forward_head(triple[0], triple[1], triple[2], segment_ids)

    attended_heads, log_total = lax.map(forward_one, (query_heads, key_heads, value_heads))
    attended = join_heads(attended_heads)

    padded = jnp.pad(emg_signal, ((0, 0), (REACH, REACH)))
    filtered = jnp.zeros((CHANNELS, TOKENS), jnp.float32)
    for tap_index in range(TAPS):
        filtered = filtered + stencil_taps[tap_index].astype(jnp.float32) * padded[:, tap_index:tap_index + TOKENS].astype(jnp.float32)
    filtered = filtered.astype(jnp.bfloat16)

    layer_out = (jnp.dot(attended, out_weight, preferred_element_type=jnp.float32)
                 + jnp.dot(filtered.T, emg_weight, preferred_element_type=jnp.float32)).astype(jnp.bfloat16)

    attn_grad = jnp.dot(out_grad, out_weight.T, preferred_element_type=jnp.float32).astype(jnp.bfloat16)
    filter_grad = jnp.dot(emg_weight, out_grad.T, preferred_element_type=jnp.float32).astype(jnp.bfloat16)
    grad_heads = split_heads(attn_grad)
    row_delta = jnp.sum(grad_heads.astype(jnp.float32) * attended_heads.astype(jnp.float32), axis=2)

    def backward_one(bundle):
        return backward_head(bundle[0], bundle[1], bundle[2], bundle[3], bundle[4], bundle[5], segment_ids)

    query_grad, key_grad, value_grad = lax.map(backward_one, (query_heads, key_heads, value_heads, grad_heads, log_total, row_delta))

    grad_pad = jnp.pad(filter_grad, ((0, 0), (REACH, REACH)))
    taps_pad = jnp.pad(stencil_taps, ((0, 0), (0, 0), (REACH, REACH)))
    emg_acc = jnp.zeros((CHANNELS, TOKENS), jnp.float32)
    for tap_index in range(TAPS):
        lower_edge = 2 * REACH - tap_index
        emg_acc = emg_acc + taps_pad[tap_index, :, lower_edge:lower_edge + TOKENS].astype(jnp.float32) * grad_pad[:, lower_edge:lower_edge + TOKENS].astype(jnp.float32)
    grad_emg = emg_acc.astype(jnp.bfloat16)
    return (layer_out, join_heads(query_grad), join_heads(key_grad), join_heads(value_grad), grad_emg)
```

```python
import functools
import math

import jax
import jax.numpy as jnp
from jax import lax
from jax.experimental import pallas as pl
from jax.experimental.pallas import tpu as pltpu
from jax.sharding import PartitionSpec as P

DH = 128
REACH = 2
TAPS = 5
MAX_SEG = 256
EDGE = 128
MASKED = -1e30
LOG2E = math.log2(math.e)
MESH = pl.DeviceIdType.MESH
BF16 = jnp.bfloat16
F32 = jnp.float32


def dot(a, b, ca=1, cb=0):
    return lax.dot_general(a, b, (((ca,), (cb,)), ((), ())), preferred_element_type=F32)


def kernel(
    n, m, hc, g,
    q_ref, k_ref, v_ref, segq_ref, segk_ref, w_ref, emg_ref, taps_ref, ew_ref, do_ref,
    out_ref, dq_ref, dk_ref, dv_ref, demg_ref,
    qg, kg, vg, kt, vt, og, lse_s, ar, po, pr, dg, acc_s, ag, dog,
    dka, dva, dqs, dks, dvs, dkr, dvr, emg_pad, taps_pad, fg_pad,
    s_in, r_in, s_ar, r_ar, s_dg, r_dg, s_po, r_po, s_do, r_do,
    s_dq, r_dq, s_kv, r_kv, s_halo, r_halo,
):
    me = lax.axis_index("ctx")
    hd = lax.axis_index("head")
    tok = q_ref.shape[0]
    tile = tok // g
    colw = do_ref.shape[1]
    my_h, my_s = me // g, me % g
    scale = DH ** (-0.5)

    def cols(h):
        return pl.ds(pl.multiple_of(h * DH, DH), DH)

    def rows(s):
        return pl.ds(pl.multiple_of(s * tile, tile), tile)

    def wide(d):
        return pl.ds(pl.multiple_of(d * colw, colw), colw)

    def remote(src, dst, ssem, rsem, **target):
        return pltpu.make_async_remote_copy(
            src_ref=src, dst_ref=dst, send_sem=ssem, recv_sem=rsem,
            device_id=target, device_id_type=MESH,
        )

    barrier = pltpu.get_barrier_semaphore()

    @pl.loop(1, n)
    def _(d):
        pl.semaphore_signal(barrier, inc=1, device_id={"ctx": (me + d) % n}, device_id_type=MESH)

    @pl.loop(1, m)
    def _(d):
        pl.semaphore_signal(barrier, inc=1, device_id={"head": (hd + d) % m}, device_id_type=MESH)

    pl.semaphore_wait(barrier, n - 1 + m - 1)

    def in_copies(t, src):
        h, s = t // g, t % g
        return (
            remote(k_ref.at[:, cols(h)], kg.at[src], s_in.at[0, t], r_in.at[0, src], ctx=t),
            remote(q_ref.at[rows(s), cols(h)], qg.at[src], s_in.at[1, t], r_in.at[1, src], ctx=t),
            remote(v_ref.at[:, cols(h)], vg.at[src], s_in.at[2, t], r_in.at[2, src], ctx=t),
        )

    def dg_copy(t, src):
        return remote(do_ref, dg.at[src], s_dg.at[t], r_dg.at[src], head=t)

    def po_copy(t, src):
        return remote(po.at[t], pr.at[src], s_po.at[t], r_po.at[src], head=t)

    def do_copy(t, src):
        return remote(ag.at[rows(t % g), cols(t // g)], dog.at[src], s_do.at[t], r_do.at[src], ctx=t)

    def ar_copy(t, src):
        return remote(og.at[t], ar.at[rows(src % g), cols(src // g)], s_ar.at[t], r_ar.at[src], ctx=t)

    def dq_copy(t, src):
        return remote(dqs.at[t], dq_ref.at[rows(src % g), cols(src // g)], s_dq.at[t], r_dq.at[src], ctx=t)

    def kv_copies(t, src):
        return (
            remote(dks.at[t], dkr.at[src], s_kv.at[0, t], r_kv.at[0, src], ctx=t),
            remote(dvs.at[t], dvr.at[src], s_kv.at[1, t], r_kv.at[1, src], ctx=t),
        )

    right, left = (me + 1) % n, (me + n - 1) % n
    last = EDGE + tok

    def halo_copies(index, pad, lead):
        def at(lo):
            return pad.at[lead + (slice(None), pl.ds(lo, EDGE))]

        return (
            remote(at(last - EDGE), at(0), s_halo.at[index, 0], r_halo.at[index, 0], ctx=right),
            remote(at(EDGE), at(last), s_halo.at[index, 1], r_halo.at[index, 1], ctx=left),
        )

    @pl.loop(1, m)
    def _(d):
        dg_copy((hd + d) % m, hd).start()

    @pl.loop(1, n)
    def _(d):
        for copy in in_copies((me + d) % n, me):
            copy.start()

    kg[me] = k_ref[:, cols(my_h)]
    vg[me] = v_ref[:, cols(my_h)]
    qg[me] = q_ref[rows(my_s), cols(my_h)]
    dg[hd] = do_ref[...]
    emg_pad[:, EDGE:last] = emg_ref[...]
    taps_pad[:, :, EDGE:last] = taps_ref[...]
    halos = halo_copies(0, emg_pad, ()) + halo_copies(1, taps_pad, (slice(None),))
    for copy in halos:
        copy.start()
    dka[...] = jnp.zeros_like(dka)
    dva[...] = jnp.zeros_like(dva)

    def arrive(b):
        @pl.when(b != me)
        def _():
            for copy in in_copies(me, b):
                copy.wait_recv()

        kt[b] = kg[b].T
        vt[b] = vg[b].T

    half = min(MAX_SEG, tok)
    need_next = ((my_s + 1) * tile + MAX_SEG - 1 > tok).astype(jnp.int32)

    def scores_of(b, c, count, masked, q):
        st = dot(kg[c, pl.ds(0, count), :], q, 1, 1) * (scale * LOG2E)
        if masked:
            segq = segq_ref[b * g + my_s]
            segk = segk_ref[c, pl.ds(0, count), :]
            st = jnp.where(segk <= segq, st, MASKED)
        return st

    def extra_of(b):
        return jnp.where(b + 1 < n, need_next, 0)

    arrive(0)

    def forward_tile(b, unused):
        @pl.when(b + 1 < n)
        def _():
            arrive(b + 1)

        q = qg[b]

        def step(c, state, count=tok, masked=False):
            top, total, acc = state
            st = scores_of(b, c, count, masked, q)
            new_top = jnp.maximum(top, jnp.max(st, axis=0, keepdims=True))
            p = jnp.exp2(st - new_top)
            factor = jnp.exp2(top - new_top)
            total = total * factor + jnp.sum(p, axis=0, keepdims=True)
            acc = acc * factor + dot(vt[c, :, pl.ds(0, count)], p.astype(BF16))
            return new_top, total, acc

        state = (
            jnp.full((1, tile), MASKED, F32),
            jnp.zeros((1, tile), F32),
            jnp.zeros((DH, tile), F32),
        )
        state = lax.fori_loop(0, b, step, state)
        state = step(b, state, masked=True)
        state = lax.fori_loop(
            0, extra_of(b), lambda i, s: step(b + 1, s, count=half, masked=True), state
        )
        top, total, acc = state
        lse_s[b] = top + jnp.log2(total)
        result = (acc / total).T.astype(BF16)
        og[b] = result

        @pl.when(b == me)
        def _():
            ar[rows(my_s), cols(my_h)] = result

        @pl.when(b != me)
        def _():
            ar_copy(b, me).start()

        return unused

    lax.fori_loop(0, n, forward_tile, 0)

    @pl.loop(1, n)
    def _(d):
        ar_copy(me, (me + d) % n).wait_recv()

    @pl.loop(1, m + 1)
    def _(d):
        t = (hd + d) % m
        part = dot(ar[...], w_ref[:, wide(t)]).astype(BF16)

        @pl.when(t == hd)
        def _():
            pr[hd] = part

        @pl.when(t != hd)
        def _():
            po[t] = part
            po_copy(t, hd).start()

    acc_s[...] = jnp.zeros_like(acc_s)
    channels = ew_ref.shape[0]

    def grad_turn(d, filter_acc):
        src = (hd + d) % m

        @pl.when(d > 0)
        def _():
            dg_copy(hd, src).wait_recv()

        block = dg[src]
        acc_s[...] += dot(block, w_ref[:, wide(src)], 1, 1)
        return filter_acc + dot(ew_ref[:, wide(src)], block, 1, 1)

    filter_acc = lax.fori_loop(0, m, grad_turn, jnp.zeros((channels, tok), F32))
    ag[...] = acc_s[...].astype(BF16)

    @pl.loop(1, n)
    def _(d):
        do_copy((me + d) % n, me).start()

    dog[me] = ag[rows(my_s), cols(my_h)]
    fg_pad[:, EDGE:last] = filter_acc.astype(BF16)
    fg_halos = halo_copies(2, fg_pad, ())
    for copy in fg_halos:
        copy.start()

    def send_kv(c):
        key_part, value_part = dka[c].astype(BF16), dva[c].astype(BF16)

        @pl.when(c == me)
        def _():
            dkr[me] = key_part
            dvr[me] = value_part

        @pl.when(c != me)
        def _():
            dks[c] = key_part
            dvs[c] = value_part
            for copy in kv_copies(c, me):
                copy.start()

    def backward_tile(turn, unused):
        b = n - 1 - turn

        @pl.when(b != me)
        def _():
            do_copy(me, b).wait_recv()

        q, do, lse = qg[b], dog[b], lse_s[b]
        delta = jnp.sum((do.astype(F32) * og[b].astype(F32)).T, axis=0, keepdims=True)

        def step(c, dqt, count=tok, masked=False):
            keys = pl.ds(0, count)
            st = scores_of(b, c, count, masked, q)
            p = jnp.exp2(st - lse)
            dpt = dot(vg[c, keys, :], do, 1, 1)
            ds = (p * (dpt - delta)).astype(BF16)
            dva[c, keys, :] += dot(p.astype(BF16), do)
            dka[c, keys, :] += dot(ds, q)
            return dqt + dot(kt[c, :, keys], ds)

        dqt = lax.fori_loop(
            0, extra_of(b), lambda i, s: step(b + 1, s, count=half, masked=True),
            jnp.zeros((DH, tile), F32),
        )

        @pl.when(b + 1 < n)
        def _():
            send_kv(b + 1)

        dqt = step(b, dqt, masked=True)
        dqt = lax.fori_loop(0, b, step, dqt)
        result = (dqt * scale).T.astype(BF16)

        @pl.when(b == me)
        def _():
            dq_ref[rows(my_s), cols(my_h)] = result

        @pl.when(b != me)
        def _():
            dqs[b] = result
            dq_copy(b, me).start()

        return unused

    lax.fori_loop(0, n, backward_tile, 0)
    send_kv(0)

    for copy in halos + fg_halos:
        copy.wait_recv()

    span = tok + 2 * EDGE
    frame = lax.broadcasted_iota(jnp.int32, (channels, span), 1) + me * tok - EDGE
    inside = (frame >= 0) & (frame < n * tok)
    emg_all = jnp.where(inside, emg_pad[...].astype(F32), 0.0)
    fg_all = jnp.where(inside, fg_pad[...].astype(F32), 0.0)
    filtered = jnp.zeros((channels, tok), F32)
    emg_acc = jnp.zeros((channels, tok), F32)
    for j in range(TAPS):
        tap = taps_pad[j].astype(F32)
        moved = pltpu.roll(emg_all, (REACH - j) % span, 1)
        filtered = filtered + (tap * moved)[:, EDGE:last]
        prod = jnp.where(inside, tap * fg_all, 0.0)
        emg_acc = emg_acc + pltpu.roll(prod, (j - REACH) % span, 1)[:, EDGE:last]
    demg_ref[...] = emg_acc.astype(BF16)
    rows_filtered = filtered.T.astype(BF16)

    @pl.loop(1, m)
    def _(d):
        po_copy(hd, (hd + d) % m).wait_recv()

    total = dot(rows_filtered, ew_ref[:, wide(hd)])
    for d in range(m):
        total = total + pr[d].astype(F32)
    out_ref[...] = total.astype(BF16)

    @pl.loop(1, n)
    def _(d):
        src = (me + d) % n
        dq_copy(me, src).wait_recv()
        for copy in kv_copies(me, src):
            copy.wait_recv()

    for h in range(hc):
        key_sum = jnp.zeros((tok, DH), F32)
        value_sum = jnp.zeros((tok, DH), F32)
        for s in range(g):
            key_sum = key_sum + dkr[h * g + s].astype(F32)
            value_sum = value_sum + dvr[h * g + s].astype(F32)
        dk_ref[:, h * DH:(h + 1) * DH] = (key_sum * scale).astype(BF16)
        dv_ref[:, h * DH:(h + 1) * DH] = value_sum.astype(BF16)

    @pl.loop(1, n)
    def _(d):
        t = (me + d) % n
        for copy in in_copies(t, me) + kv_copies(t, me):
            copy.wait_send()
        ar_copy(t, me).wait_send()
        do_copy(t, me).wait_send()
        dq_copy(t, me).wait_send()

    @pl.loop(1, m)
    def _(d):
        t = (hd + d) % m
        dg_copy(t, hd).wait_send()
        po_copy(t, hd).wait_send()

    for copy in halos + fg_halos:
        copy.wait_send()


def body(n, m, q, k, v, seg, w, emg, taps, ew, do):
    tok, width = q.shape
    hc = width // DH
    g = n // hc
    tile = tok // g
    colw = do.shape[1]
    ch = ew.shape[0]
    span = tok + 2 * EDGE
    segq = seg.reshape(n * g, 1, tile)
    segk = seg.reshape(n, tok, 1)
    vmem = pl.BlockSpec(memory_space=pltpu.VMEM)
    dma = pltpu.SemaphoreType.DMA

    def buf(shape, dtype=BF16):
        return pltpu.VMEM(shape, dtype)

    scratch = [
        buf((n, tile, DH)), buf((n, tok, DH)), buf((n, tok, DH)),
        buf((n, DH, tok)), buf((n, DH, tok)),
        buf((n, tile, DH)), buf((n, 1, tile), F32), buf((tok, width)),
        buf((m, tok, colw)), buf((m, tok, colw)), buf((m, tok, colw)),
        buf((tok, width), F32), buf((tok, width)), buf((n, tile, DH)),
        buf((n, tok, DH), F32), buf((n, tok, DH), F32),
        buf((n, tile, DH)), buf((n, tok, DH)), buf((n, tok, DH)),
        buf((n, tok, DH)), buf((n, tok, DH)),
        buf((ch, span)), buf((TAPS, ch, span)), buf((ch, span)),
        dma((3, n)), dma((3, n)), dma((n,)), dma((n,)), dma((m,)), dma((m,)),
        dma((m,)), dma((m,)), dma((n,)), dma((n,)), dma((n,)), dma((n,)),
        dma((2, n)), dma((2, n)), dma((3, 2)), dma((3, 2)),
    ]
    shapes = [(tok, colw), (tok, width), (tok, width), (tok, width), (ch, tok)]
    return tuple(pl.pallas_call(
        functools.partial(kernel, n, m, hc, g),
        out_shape=[jax.ShapeDtypeStruct(s, BF16) for s in shapes],
        in_specs=[vmem] * 10,
        out_specs=[vmem] * 5,
        scratch_shapes=scratch,
        compiler_params=pltpu.CompilerParams(
            collective_id=0, has_side_effects=True, vmem_limit_bytes=56 * 2**20
        ),
    )(q, k, v, segq, segk, w, emg, taps, ew, do))


def solution(mesh):
    n, m = mesh.shape["ctx"], mesh.shape["head"]
    rows = P("ctx", "head")
    in_specs = (
        rows, rows, rows, P(), P("head", None), P(None, "ctx"), P(None, None, "ctx"), P(), rows,
    )
    out_specs = (rows, rows, rows, rows, P(None, "ctx"))
    return jax.shard_map(
        functools.partial(body, n, m), mesh=mesh, in_specs=in_specs, out_specs=out_specs,
        check_vma=False,
    )
```

```python
import functools
import math

import jax
import jax.numpy as jnp
from jax import lax
from jax.experimental import pallas as pl
from jax.experimental.pallas import tpu as pltpu
from jax.sharding import PartitionSpec as P

DH = 128
REACH = 2
TAPS = 5
MAX_SEG = 256
EDGE = 128
MASKED = -1e30
LOG2E = math.log2(math.e)
MESH = pl.DeviceIdType.MESH
BF16 = jnp.bfloat16
F32 = jnp.float32


def dot(a, b, ca=1, cb=0):
    return lax.dot_general(a, b, (((ca,), (cb,)), ((), ())), preferred_element_type=F32)


def kernel(
    n, m, hc, g,
    q_ref, k_ref, v_ref, segq_ref, seg_ref, w_ref, emg_ref, taps_ref, ew_ref, do_ref,
    out_ref, dq_ref, dk_ref, dv_ref, demg_ref,
    qg, kg, vg, kt, vt, og, lse_s, ar, po, pr, dg, acc_s, ag, dog,
    dka, dva, dqs, dks, dvs, dkr, dvr, dkf, dvf, segk_ref, emg_pad, taps_pad, fg_pad,
    s_in, r_in, s_ar, r_ar, s_dg, r_dg, s_po, r_po, s_do, r_do,
    s_dq, r_dq, s_kv, r_kv, s_sib, r_sib, s_part, r_part, s_halo, r_halo,
):
    me = lax.axis_index("ctx")
    hd = lax.axis_index("head")
    tok = q_ref.shape[0]
    tile = tok // g
    colw = do_ref.shape[1]
    my_h, my_s = me // g, me % g
    scale = DH ** (-0.5)

    def cols(h):
        return pl.ds(pl.multiple_of(h * DH, DH), DH)

    def rows(s):
        return pl.ds(pl.multiple_of(s * tile, tile), tile)

    def wide(d):
        return pl.ds(pl.multiple_of(d * colw, colw), colw)

    def remote(src, dst, ssem, rsem, **target):
        return pltpu.make_async_remote_copy(
            src_ref=src, dst_ref=dst, send_sem=ssem, recv_sem=rsem,
            device_id=target, device_id_type=MESH,
        )

    barrier = pltpu.get_barrier_semaphore()

    @pl.loop(1, n)
    def _(d):
        pl.semaphore_signal(barrier, inc=1, device_id={"ctx": (me + d) % n}, device_id_type=MESH)

    @pl.loop(1, m)
    def _(d):
        pl.semaphore_signal(barrier, inc=1, device_id={"head": (hd + d) % m}, device_id_type=MESH)

    pl.semaphore_wait(barrier, n - 1 + m - 1)

    def in_copies(t, src):
        h, s = t // g, t % g
        return (
            remote(k_ref.at[rows(s), cols(h)], kg.at[src, rows(s)], s_in.at[0, t], r_in.at[0, src], ctx=t),
            remote(q_ref.at[rows(s), cols(h)], qg.at[src], s_in.at[1, t], r_in.at[1, src], ctx=t),
            remote(v_ref.at[rows(s), cols(h)], vg.at[src, rows(s)], s_in.at[2, t], r_in.at[2, src], ctx=t),
        )

    def dg_copy(t, src):
        return remote(do_ref, dg.at[src], s_dg.at[t], r_dg.at[src], head=t)

    def po_copy(t, src):
        return remote(po.at[t], pr.at[src], s_po.at[t], r_po.at[src], head=t)

    def do_copy(t, src):
        return remote(ag.at[rows(t % g), cols(t // g)], dog.at[src], s_do.at[t], r_do.at[src], ctx=t)

    def ar_copy(t, src):
        return remote(og.at[t], ar.at[rows(src % g), cols(src // g)], s_ar.at[t], r_ar.at[src], ctx=t)

    def dq_copy(t, src):
        return remote(dqs.at[t], dq_ref.at[rows(src % g), cols(src // g)], s_dq.at[t], r_dq.at[src], ctx=t)

    def kv_copies(t, src):
        return (
            remote(dkf.at[t], dk_ref.at[rows(src % g), cols(src // g)], s_kv.at[0, t], r_kv.at[0, src], ctx=t),
            remote(dvf.at[t], dv_ref.at[rows(src % g), cols(src // g)], s_kv.at[1, t], r_kv.at[1, src], ctx=t),
        )

    def sib_copies(to, frm, b):
        return tuple(
            remote(ref.at[b, rows(frm)], ref.at[b, rows(frm)], s_sib.at[i, to, b], r_sib.at[i, frm, b],
                   ctx=my_h * g + to)
            for i, ref in enumerate((kg, vg))
        )

    def part_copies(to, frm, c):
        return tuple(
            remote(src.at[c, rows(to)], dst.at[c, frm], s_part.at[i, to, c], r_part.at[i, frm, c],
                   ctx=my_h * g + to)
            for i, (src, dst) in enumerate(((dks, dkr), (dvs, dvr)))
        )

    right, left = (me + 1) % n, (me + n - 1) % n
    last = EDGE + tok

    def halo_copies(index, pad, lead):
        def at(lo):
            return pad.at[lead + (slice(None), pl.ds(lo, EDGE))]

        return (
            remote(at(last - EDGE), at(0), s_halo.at[index, 0], r_halo.at[index, 0], ctx=right),
            remote(at(EDGE), at(last), s_halo.at[index, 1], r_halo.at[index, 1], ctx=left),
        )

    @pl.loop(1, m)
    def _(d):
        dg_copy((hd + d) % m, hd).start()

    @pl.loop(1, n)
    def _(d):
        for copy in in_copies((me + d) % n, me):
            copy.start()

    kg[me, rows(my_s), :] = k_ref[rows(my_s), cols(my_h)]
    vg[me, rows(my_s), :] = v_ref[rows(my_s), cols(my_h)]
    qg[me] = q_ref[rows(my_s), cols(my_h)]
    dg[hd] = do_ref[...]
    emg_pad[:, EDGE:last] = emg_ref[...]
    taps_pad[:, :, EDGE:last] = taps_ref[...]
    halos = halo_copies(0, emg_pad, ()) + halo_copies(1, taps_pad, (slice(None),))
    for copy in halos:
        copy.start()
    dka[...] = jnp.zeros_like(dka)
    dva[...] = jnp.zeros_like(dva)

    @pl.loop(0, n)
    def _(c):
        segk_ref[c] = jnp.broadcast_to(seg_ref[c], (8, tok)).T[:, :1]

    def pass_on(b):
        @pl.when(b != me)
        def _():
            for copy in in_copies(me, b):
                copy.wait_recv()

        @pl.loop(1, g)
        def _(d):
            for copy in sib_copies((my_s + d) % g, my_s, b):
                copy.start()

    def arrive(b):
        @pl.loop(1, g)
        def _(d):
            for copy in sib_copies(my_s, (my_s + d) % g, b):
                copy.wait_recv()

        kt[b] = kg[b].T
        vt[b] = vg[b].T

    half = min(MAX_SEG, tok)
    need_next = ((my_s + 1) * tile + MAX_SEG - 1 > tok).astype(jnp.int32)

    def scores_of(b, c, count, masked, q):
        st = dot(kg[c, pl.ds(0, count), :], q, 1, 1) * (scale * LOG2E)
        if masked:
            segq = segq_ref[b * g + my_s]
            segk = segk_ref[c, pl.ds(0, count), :]
            st = jnp.where(segk <= segq, st, MASKED)
        return st

    def extra_of(b):
        return jnp.where(b + 1 < n, need_next, 0)

    pass_on(0)
    pass_on(1)
    arrive(0)

    def forward_tile(b, unused):
        @pl.when(b + 2 < n)
        def _():
            pass_on(b + 2)

        @pl.when(b + 1 < n)
        def _():
            arrive(b + 1)

        q = qg[b]

        def step(c, state, count=tok, masked=False):
            top, total, acc = state
            st = scores_of(b, c, count, masked, q)
            new_top = jnp.maximum(top, jnp.max(st, axis=0, keepdims=True))
            p = jnp.exp2(st - new_top)
            factor = jnp.exp2(top - new_top)
            total = total * factor + jnp.sum(p, axis=0, keepdims=True)
            acc = acc * factor + dot(vt[c, :, pl.ds(0, count)], p.astype(BF16))
            return new_top, total, acc

        state = (
            jnp.full((1, tile), MASKED, F32),
            jnp.zeros((1, tile), F32),
            jnp.zeros((DH, tile), F32),
        )
        state = lax.fori_loop(0, b, step, state)
        state = step(b, state, masked=True)
        state = lax.fori_loop(
            0, extra_of(b), lambda i, s: step(b + 1, s, count=half, masked=True), state
        )
        top, total, acc = state
        lse_s[b] = top + jnp.log2(total)
        result = (acc / total).T.astype(BF16)
        og[b] = result

        @pl.when(b == me)
        def _():
            ar[rows(my_s), cols(my_h)] = result

        @pl.when(b != me)
        def _():
            ar_copy(b, me).start()

        return unused

    lax.fori_loop(0, n, forward_tile, 0)

    @pl.loop(1, n)
    def _(d):
        ar_copy(me, (me + d) % n).wait_recv()

    @pl.loop(1, m + 1)
    def _(d):
        t = (hd + d) % m
        part = dot(ar[...], w_ref[:, wide(t)]).astype(BF16)

        @pl.when(t == hd)
        def _():
            pr[hd] = part

        @pl.when(t != hd)
        def _():
            po[t] = part
            po_copy(t, hd).start()

    acc_s[...] = jnp.zeros_like(acc_s)
    channels = ew_ref.shape[0]

    def grad_turn(d, filter_acc):
        src = (hd + d) % m

        @pl.when(d > 0)
        def _():
            dg_copy(hd, src).wait_recv()

        block = dg[src]
        acc_s[...] += dot(block, w_ref[:, wide(src)], 1, 1)
        return filter_acc + dot(ew_ref[:, wide(src)], block, 1, 1)

    filter_acc = lax.fori_loop(0, m, grad_turn, jnp.zeros((channels, tok), F32))
    ag[...] = acc_s[...].astype(BF16)

    @pl.loop(1, n)
    def _(d):
        do_copy((me + d) % n, me).start()

    dog[me] = ag[rows(my_s), cols(my_h)]
    fg_pad[:, EDGE:last] = filter_acc.astype(BF16)
    fg_halos = halo_copies(2, fg_pad, ())
    for copy in fg_halos:
        copy.start()

    def send_parts(c):
        dks[c] = dka[c].astype(BF16)
        dvs[c] = dva[c].astype(BF16)

        @pl.loop(1, g)
        def _(d):
            for copy in part_copies((my_s + d) % g, my_s, c):
                copy.start()

    def send_kv(c):
        def add(d, sums):
            frm = (my_s + d) % g
            for copy in part_copies(my_s, frm, c):
                copy.wait_recv()
            return sums[0] + dkr[c, frm].astype(F32), sums[1] + dvr[c, frm].astype(F32)

        sums = lax.fori_loop(1, g, add, (dka[c, rows(my_s), :], dva[c, rows(my_s), :]))
        key_part, value_part = (sums[0] * scale).astype(BF16), sums[1].astype(BF16)

        @pl.when(c == me)
        def _():
            dk_ref[rows(my_s), cols(my_h)] = key_part
            dv_ref[rows(my_s), cols(my_h)] = value_part

        @pl.when(c != me)
        def _():
            dkf[c] = key_part
            dvf[c] = value_part
            for copy in kv_copies(c, me):
                copy.start()

    def backward_tile(turn, unused):
        b = n - 1 - turn

        @pl.when(b != me)
        def _():
            do_copy(me, b).wait_recv()

        q, do, lse = qg[b], dog[b], lse_s[b]
        delta = jnp.sum((do.astype(F32) * og[b].astype(F32)).T, axis=0, keepdims=True)

        def step(c, dqt, count=tok, masked=False):
            keys = pl.ds(0, count)
            st = scores_of(b, c, count, masked, q)
            p = jnp.exp2(st - lse)
            dpt = dot(vg[c, keys, :], do, 1, 1)
            ds = (p * (dpt - delta)).astype(BF16)
            dva[c, keys, :] += dot(p.astype(BF16), do)
            dka[c, keys, :] += dot(ds, q)
            return dqt + dot(kt[c, :, keys], ds)

        dqt = lax.fori_loop(
            0, extra_of(b), lambda i, s: step(b + 1, s, count=half, masked=True),
            jnp.zeros((DH, tile), F32),
        )

        @pl.when(b + 1 < n)
        def _():
            send_parts(b + 1)

        dqt = step(b, dqt, masked=True)
        dqt = lax.fori_loop(0, b, step, dqt)
        result = (dqt * scale).T.astype(BF16)

        @pl.when(b == me)
        def _():
            dq_ref[rows(my_s), cols(my_h)] = result

        @pl.when(b != me)
        def _():
            dqs[b] = result
            dq_copy(b, me).start()

        @pl.when(b + 1 < n)
        def _():
            send_kv(b + 1)

        return unused

    lax.fori_loop(0, n, backward_tile, 0)
    send_parts(0)
    send_kv(0)

    for copy in halos + fg_halos:
        copy.wait_recv()

    span = tok + 2 * EDGE
    frame = lax.broadcasted_iota(jnp.int32, (channels, span), 1) + me * tok - EDGE
    inside = (frame >= 0) & (frame < n * tok)
    emg_all = jnp.where(inside, emg_pad[...].astype(F32), 0.0)
    fg_all = jnp.where(inside, fg_pad[...].astype(F32), 0.0)
    filtered = jnp.zeros((channels, tok), F32)
    emg_acc = jnp.zeros((channels, tok), F32)
    for j in range(TAPS):
        tap = taps_pad[j].astype(F32)
        moved = pltpu.roll(emg_all, (REACH - j) % span, 1)
        filtered = filtered + (tap * moved)[:, EDGE:last]
        prod = jnp.where(inside, tap * fg_all, 0.0)
        emg_acc = emg_acc + pltpu.roll(prod, (j - REACH) % span, 1)[:, EDGE:last]
    demg_ref[...] = emg_acc.astype(BF16)
    rows_filtered = filtered.T.astype(BF16)

    @pl.loop(1, m)
    def _(d):
        po_copy(hd, (hd + d) % m).wait_recv()

    total = dot(rows_filtered, ew_ref[:, wide(hd)])
    for d in range(m):
        total = total + pr[d].astype(F32)
    out_ref[...] = total.astype(BF16)

    @pl.loop(1, n)
    def _(d):
        src = (me + d) % n
        dq_copy(me, src).wait_recv()
        for copy in kv_copies(me, src):
            copy.wait_recv()

    @pl.loop(1, g)
    def _(d):
        to = (my_s + d) % g

        @pl.loop(0, n)
        def _(b):
            for copy in sib_copies(to, my_s, b) + part_copies(to, my_s, b):
                copy.wait_send()

    @pl.loop(1, n)
    def _(d):
        t = (me + d) % n
        for copy in in_copies(t, me) + kv_copies(t, me):
            copy.wait_send()
        ar_copy(t, me).wait_send()
        do_copy(t, me).wait_send()
        dq_copy(t, me).wait_send()

    @pl.loop(1, m)
    def _(d):
        t = (hd + d) % m
        dg_copy(t, hd).wait_send()
        po_copy(t, hd).wait_send()

    for copy in halos + fg_halos:
        copy.wait_send()


def body(n, m, q, k, v, seg, w, emg, taps, ew, do):
    tok, width = q.shape
    hc = width // DH
    g = n // hc
    tile = tok // g
    colw = do.shape[1]
    ch = ew.shape[0]
    span = tok + 2 * EDGE
    segq = seg.reshape(n * g, 1, tile)
    segk = seg.reshape(n, 1, tok)
    vmem = pl.BlockSpec(memory_space=pltpu.VMEM)
    dma = pltpu.SemaphoreType.DMA

    def buf(shape, dtype=BF16):
        return pltpu.VMEM(shape, dtype)

    scratch = [
        buf((n, tile, DH)), buf((n, tok, DH)), buf((n, tok, DH)),
        buf((n, DH, tok)), buf((n, DH, tok)),
        buf((n, tile, DH)), buf((n, 1, tile), F32), buf((tok, width)),
        buf((m, tok, colw)), buf((m, tok, colw)), buf((m, tok, colw)),
        buf((tok, width), F32), buf((tok, width)), buf((n, tile, DH)),
        buf((n, tok, DH), F32), buf((n, tok, DH), F32),
        buf((n, tile, DH)), buf((n, tok, DH)), buf((n, tok, DH)),
        buf((n, g, tile, DH)), buf((n, g, tile, DH)),
        buf((n, tile, DH)), buf((n, tile, DH)), buf((n, tok, 1), jnp.int32),
        buf((ch, span)), buf((TAPS, ch, span)), buf((ch, span)),
        dma((3, n)), dma((3, n)), dma((n,)), dma((n,)), dma((m,)), dma((m,)),
        dma((m,)), dma((m,)), dma((n,)), dma((n,)), dma((n,)), dma((n,)),
        dma((2, n)), dma((2, n)), dma((2, g, n)), dma((2, g, n)), dma((2, g, n)), dma((2, g, n)), dma((3, 2)), dma((3, 2)),
    ]
    shapes = [(tok, colw), (tok, width), (tok, width), (tok, width), (ch, tok)]
    return tuple(pl.pallas_call(
        functools.partial(kernel, n, m, hc, g),
        out_shape=[jax.ShapeDtypeStruct(s, BF16) for s in shapes],
        in_specs=[vmem] * 10,
        out_specs=[vmem] * 5,
        scratch_shapes=scratch,
        compiler_params=pltpu.CompilerParams(
            collective_id=0, has_side_effects=True, vmem_limit_bytes=56 * 2**20
        ),
    )(q, k, v, segq, segk, w, emg, taps, ew, do))


def solution(mesh):
    n, m = mesh.shape["ctx"], mesh.shape["head"]
    rows = P("ctx", "head")
    in_specs = (
        rows, rows, rows, P(), P("head", None), P(None, "ctx"), P(None, None, "ctx"), P(), rows,
    )
    out_specs = (rows, rows, rows, rows, P(None, "ctx"))
    return jax.shard_map(
        functools.partial(body, n, m), mesh=mesh, in_specs=in_specs, out_specs=out_specs,
        check_vma=False,
    )
```

```python
import functools
import math

import jax
import jax.numpy as jnp
from jax import lax
from jax.experimental import pallas as pl
from jax.experimental.pallas import tpu as pltpu
from jax.sharding import PartitionSpec as P

DH = 128
REACH = 2
TAPS = 5
MAX_SEG = 256
EDGE = 128
MASKED = -1e30
LOG2E = math.log2(math.e)
MESH = pl.DeviceIdType.MESH
BF16 = jnp.bfloat16
F32 = jnp.float32


def dot(a, b, ca=1, cb=0):
    return lax.dot_general(a, b, (((ca,), (cb,)), ((), ())), preferred_element_type=F32)


def kernel(
    n, m, hc, g,
    q_ref, k_ref, v_ref, segq_ref, seg_ref, w_ref, emg_ref, taps_ref, ew_ref, do_ref,
    out_ref, dq_ref, dk_ref, dv_ref, demg_ref,
    qg, kg, vg, kt, vt, og, lse_s, ar, po, pr, dg, acc_s, ag, dog,
    dka, dva, dqs, dks, dvs, dkr, dvr, dkf, dvf, dqa, delta_s, segk_ref, emg_pad, taps_pad, fg_pad,
    s_in, r_in, s_ar, r_ar, s_dg, r_dg, s_po, r_po, s_do, r_do,
    s_dq, r_dq, s_kv, r_kv, s_sib, r_sib, s_part, r_part, s_halo, r_halo,
):
    me = lax.axis_index("ctx")
    hd = lax.axis_index("head")
    tok = q_ref.shape[0]
    tile = tok // g
    colw = do_ref.shape[1]
    my_h, my_s = me // g, me % g
    scale = DH ** (-0.5)

    def cols(h):
        return pl.ds(pl.multiple_of(h * DH, DH), DH)

    def rows(s):
        return pl.ds(pl.multiple_of(s * tile, tile), tile)

    def wide(d):
        return pl.ds(pl.multiple_of(d * colw, colw), colw)

    def remote(src, dst, ssem, rsem, **target):
        return pltpu.make_async_remote_copy(
            src_ref=src, dst_ref=dst, send_sem=ssem, recv_sem=rsem,
            device_id=target, device_id_type=MESH,
        )

    barrier = pltpu.get_barrier_semaphore()

    @pl.loop(1, n)
    def _(d):
        pl.semaphore_signal(barrier, inc=1, device_id={"ctx": (me + d) % n}, device_id_type=MESH)

    @pl.loop(1, m)
    def _(d):
        pl.semaphore_signal(barrier, inc=1, device_id={"head": (hd + d) % m}, device_id_type=MESH)

    pl.semaphore_wait(barrier, n - 1 + m - 1)

    def in_copies(t, src):
        h, s = t // g, t % g
        return (
            remote(k_ref.at[rows(s), cols(h)], kg.at[src, rows(s)], s_in.at[0, t], r_in.at[0, src], ctx=t),
            remote(q_ref.at[rows(s), cols(h)], qg.at[src], s_in.at[1, t], r_in.at[1, src], ctx=t),
            remote(v_ref.at[rows(s), cols(h)], vg.at[src, rows(s)], s_in.at[2, t], r_in.at[2, src], ctx=t),
        )

    def dg_copy(t, src):
        return remote(do_ref, dg.at[src], s_dg.at[t], r_dg.at[src], head=t)

    def po_copy(t, src):
        return remote(po.at[t], pr.at[src], s_po.at[t], r_po.at[src], head=t)

    def do_copy(t, src):
        return remote(ag.at[rows(t % g), cols(t // g)], dog.at[src], s_do.at[t], r_do.at[src], ctx=t)

    def ar_copy(t, src):
        return remote(og.at[t], ar.at[rows(src % g), cols(src // g)], s_ar.at[t], r_ar.at[src], ctx=t)

    def dq_copy(t, src):
        return remote(dqs.at[t], dq_ref.at[rows(src % g), cols(src // g)], s_dq.at[t], r_dq.at[src], ctx=t)

    def kv_copies(t, src):
        return (
            remote(dkf.at[t], dk_ref.at[rows(src % g), cols(src // g)], s_kv.at[0, t], r_kv.at[0, src], ctx=t),
            remote(dvf.at[t], dv_ref.at[rows(src % g), cols(src // g)], s_kv.at[1, t], r_kv.at[1, src], ctx=t),
        )

    def sib_copies(to, frm, b):
        return tuple(
            remote(ref.at[b, rows(frm)], ref.at[b, rows(frm)], s_sib.at[i, to, b], r_sib.at[i, frm, b],
                   ctx=my_h * g + to)
            for i, ref in enumerate((kg, vg))
        )

    def part_copies(to, frm, c):
        return tuple(
            remote(src.at[c, rows(to)], dst.at[c, frm], s_part.at[i, to, c], r_part.at[i, frm, c],
                   ctx=my_h * g + to)
            for i, (src, dst) in enumerate(((dks, dkr), (dvs, dvr)))
        )

    right, left = (me + 1) % n, (me + n - 1) % n
    last = EDGE + tok

    def halo_copies(index, pad, lead):
        def at(lo):
            return pad.at[lead + (slice(None), pl.ds(lo, EDGE))]

        return (
            remote(at(last - EDGE), at(0), s_halo.at[index, 0], r_halo.at[index, 0], ctx=right),
            remote(at(EDGE), at(last), s_halo.at[index, 1], r_halo.at[index, 1], ctx=left),
        )

    @pl.loop(1, m)
    def _(d):
        dg_copy((hd + d) % m, hd).start()

    @pl.loop(1, n)
    def _(d):
        for copy in in_copies((me + d) % n, me):
            copy.start()

    kg[me, rows(my_s), :] = k_ref[rows(my_s), cols(my_h)]
    vg[me, rows(my_s), :] = v_ref[rows(my_s), cols(my_h)]
    qg[me] = q_ref[rows(my_s), cols(my_h)]
    dg[hd] = do_ref[...]
    emg_pad[:, EDGE:last] = emg_ref[...]
    taps_pad[:, :, EDGE:last] = taps_ref[...]
    halos = halo_copies(0, emg_pad, ()) + halo_copies(1, taps_pad, (slice(None),))
    for copy in halos:
        copy.start()
    dka[...] = jnp.zeros_like(dka)
    dva[...] = jnp.zeros_like(dva)

    @pl.loop(0, n)
    def _(c):
        segk_ref[c] = jnp.broadcast_to(seg_ref[c], (8, tok)).T[:, :1]

    def pass_on(b):
        @pl.when(b != me)
        def _():
            for copy in in_copies(me, b):
                copy.wait_recv()

        @pl.loop(1, g)
        def _(d):
            for copy in sib_copies((my_s + d) % g, my_s, b):
                copy.start()

    def arrive(b):
        @pl.loop(1, g)
        def _(d):
            for copy in sib_copies(my_s, (my_s + d) % g, b):
                copy.wait_recv()

        kt[b] = kg[b].T
        vt[b] = vg[b].T

    half = min(MAX_SEG, tok)
    need_next = ((my_s + 1) * tile + MAX_SEG - 1 > tok).astype(jnp.int32)

    def scores_of(b, c, count, masked, q):
        st = dot(kg[c, pl.ds(0, count), :], q, 1, 1) * (scale * LOG2E)
        if masked:
            segq = segq_ref[b * g + my_s]
            segk = segk_ref[c, pl.ds(0, count), :]
            st = jnp.where(segk <= segq, st, MASKED)
        return st

    def extra_of(b):
        return jnp.where(b + 1 < n, need_next, 0)

    pass_on(0)
    pass_on(1)
    arrive(0)

    def forward_tile(b, unused):
        @pl.when(b + 2 < n)
        def _():
            pass_on(b + 2)

        @pl.when(b + 1 < n)
        def _():
            arrive(b + 1)

        q = qg[b]

        def step(c, state, count=tok, masked=False):
            top, total, acc = state
            st = scores_of(b, c, count, masked, q)
            new_top = jnp.maximum(top, jnp.max(st, axis=0, keepdims=True))
            p = jnp.exp2(st - new_top)
            factor = jnp.exp2(top - new_top)
            total = total * factor + jnp.sum(p, axis=0, keepdims=True)
            acc = acc * factor + dot(vt[c, :, pl.ds(0, count)], p.astype(BF16))
            return new_top, total, acc

        state = (
            jnp.full((1, tile), MASKED, F32),
            jnp.zeros((1, tile), F32),
            jnp.zeros((DH, tile), F32),
        )
        state = lax.fori_loop(0, b, step, state)
        state = step(b, state, masked=True)
        state = lax.fori_loop(
            0, extra_of(b), lambda i, s: step(b + 1, s, count=half, masked=True), state
        )
        top, total, acc = state
        lse_s[b] = top + jnp.log2(total)
        result = (acc / total).T.astype(BF16)
        og[b] = result

        @pl.when(b == me)
        def _():
            ar[rows(my_s), cols(my_h)] = result

        @pl.when(b != me)
        def _():
            ar_copy(b, me).start()

        return unused

    lax.fori_loop(0, n, forward_tile, 0)

    acc_s[...] = jnp.zeros_like(acc_s)
    channels = ew_ref.shape[0]

    def grad_turn(d, filter_acc):
        src = (hd + d) % m

        @pl.when(d > 0)
        def _():
            dg_copy(hd, src).wait_recv()

        block = dg[src]
        acc_s[...] += dot(block, w_ref[:, wide(src)], 1, 1)
        return filter_acc + dot(ew_ref[:, wide(src)], block, 1, 1)

    filter_acc = lax.fori_loop(0, m, grad_turn, jnp.zeros((channels, tok), F32))
    ag[...] = acc_s[...].astype(BF16)

    @pl.loop(1, n)
    def _(d):
        do_copy((me + d) % n, me).start()

    dog[me] = ag[rows(my_s), cols(my_h)]
    fg_pad[:, EDGE:last] = filter_acc.astype(BF16)
    fg_halos = halo_copies(2, fg_pad, ())
    for copy in fg_halos:
        copy.start()

    @pl.loop(1, n)
    def _(d):
        ar_copy(me, (me + d) % n).wait_recv()

    @pl.loop(1, m + 1)
    def _(d):
        t = (hd + d) % m
        part = dot(ar[...], w_ref[:, wide(t)]).astype(BF16)

        @pl.when(t == hd)
        def _():
            pr[hd] = part

        @pl.when(t != hd)
        def _():
            po[t] = part
            po_copy(t, hd).start()

    def send_parts(c):
        dks[c] = dka[c].astype(BF16)
        dvs[c] = dva[c].astype(BF16)

        @pl.loop(1, g)
        def _(d):
            for copy in part_copies((my_s + d) % g, my_s, c):
                copy.start()

    def send_kv(c):
        def add(d, sums):
            frm = (my_s + d) % g
            for copy in part_copies(my_s, frm, c):
                copy.wait_recv()
            return sums[0] + dkr[c, frm].astype(F32), sums[1] + dvr[c, frm].astype(F32)

        sums = lax.fori_loop(1, g, add, (dka[c, rows(my_s), :], dva[c, rows(my_s), :]))
        key_part, value_part = (sums[0] * scale).astype(BF16), sums[1].astype(BF16)

        @pl.when(c == me)
        def _():
            dk_ref[rows(my_s), cols(my_h)] = key_part
            dv_ref[rows(my_s), cols(my_h)] = value_part

        @pl.when(c != me)
        def _():
            dkf[c] = key_part
            dvf[c] = value_part
            for copy in kv_copies(c, me):
                copy.start()

    @pl.loop(0, n)
    def _(b):
        @pl.when(b != me)
        def _():
            do_copy(me, b).wait_recv()

        terms = dog[b].astype(F32) * og[b].astype(F32)
        delta_s[b] = jnp.sum(terms.T, axis=0, keepdims=True)
        dqa[b] = jnp.zeros((DH, tile), F32)

    def backward_step(c, b, count=tok, masked=False):
        keys = pl.ds(0, count)
        q, do = qg[b], dog[b]
        st = scores_of(b, c, count, masked, q)
        p = jnp.exp2(st - lse_s[b])
        dpt = dot(vg[c, keys, :], do, 1, 1)
        ds = (p * (dpt - delta_s[b])).astype(BF16)
        dva[c, keys, :] += dot(p.astype(BF16), do)
        dka[c, keys, :] += dot(ds, q)
        dqa[b] += dot(kt[c, :, keys], ds)

    def ordered(turn):
        return (turn + (my_h + 1) * g) % n

    @pl.loop(0, n)
    def _(turn):
        c = ordered(turn)

        @pl.loop(0, jnp.where(c > 0, need_next, 0))
        def _(i):
            backward_step(c, c - 1, count=half, masked=True)

        backward_step(c, c, masked=True)

        @pl.loop(c + 1, n)
        def _(b):
            backward_step(c, b)

        send_parts(c)

        @pl.when(turn > 0)
        def _():
            send_kv(ordered(turn + n - 1))

    @pl.loop(0, n)
    def _(turn):
        b = ordered(turn)
        result = (dqa[b] * scale).T.astype(BF16)

        @pl.when(b == me)
        def _():
            dq_ref[rows(my_s), cols(my_h)] = result

        @pl.when(b != me)
        def _():
            dqs[b] = result
            dq_copy(b, me).start()

    send_kv(ordered(n - 1))

    for copy in halos + fg_halos:
        copy.wait_recv()

    span = tok + 2 * EDGE
    frame = lax.broadcasted_iota(jnp.int32, (channels, span), 1) + me * tok - EDGE
    inside = (frame >= 0) & (frame < n * tok)
    emg_all = jnp.where(inside, emg_pad[...].astype(F32), 0.0)
    fg_all = jnp.where(inside, fg_pad[...].astype(F32), 0.0)
    filtered = jnp.zeros((channels, tok), F32)
    emg_acc = jnp.zeros((channels, tok), F32)
    for j in range(TAPS):
        tap = taps_pad[j].astype(F32)
        moved = pltpu.roll(emg_all, (REACH - j) % span, 1)
        filtered = filtered + (tap * moved)[:, EDGE:last]
        prod = jnp.where(inside, tap * fg_all, 0.0)
        emg_acc = emg_acc + pltpu.roll(prod, (j - REACH) % span, 1)[:, EDGE:last]
    demg_ref[...] = emg_acc.astype(BF16)
    rows_filtered = filtered.T.astype(BF16)

    @pl.loop(1, m)
    def _(d):
        po_copy(hd, (hd + d) % m).wait_recv()

    total = dot(rows_filtered, ew_ref[:, wide(hd)])
    for d in range(m):
        total = total + pr[d].astype(F32)
    out_ref[...] = total.astype(BF16)

    @pl.loop(1, n)
    def _(d):
        src = (me + d) % n
        dq_copy(me, src).wait_recv()
        for copy in kv_copies(me, src):
            copy.wait_recv()

    @pl.loop(1, g)
    def _(d):
        to = (my_s + d) % g

        @pl.loop(0, n)
        def _(b):
            for copy in sib_copies(to, my_s, b) + part_copies(to, my_s, b):
                copy.wait_send()

    @pl.loop(1, n)
    def _(d):
        t = (me + d) % n
        for copy in in_copies(t, me) + kv_copies(t, me):
            copy.wait_send()
        ar_copy(t, me).wait_send()
        do_copy(t, me).wait_send()
        dq_copy(t, me).wait_send()

    @pl.loop(1, m)
    def _(d):
        t = (hd + d) % m
        dg_copy(t, hd).wait_send()
        po_copy(t, hd).wait_send()

    for copy in halos + fg_halos:
        copy.wait_send()


def body(n, m, q, k, v, seg, w, emg, taps, ew, do):
    tok, width = q.shape
    hc = width // DH
    g = n // hc
    tile = tok // g
    colw = do.shape[1]
    ch = ew.shape[0]
    span = tok + 2 * EDGE
    segq = seg.reshape(n * g, 1, tile)
    segk = seg.reshape(n, 1, tok)
    vmem = pl.BlockSpec(memory_space=pltpu.VMEM)
    dma = pltpu.SemaphoreType.DMA

    def buf(shape, dtype=BF16):
        return pltpu.VMEM(shape, dtype)

    scratch = [
        buf((n, tile, DH)), buf((n, tok, DH)), buf((n, tok, DH)),
        buf((n, DH, tok)), buf((n, DH, tok)),
        buf((n, tile, DH)), buf((n, 1, tile), F32), buf((tok, width)),
        buf((m, tok, colw)), buf((m, tok, colw)), buf((m, tok, colw)),
        buf((tok, width), F32), buf((tok, width)), buf((n, tile, DH)),
        buf((n, tok, DH), F32), buf((n, tok, DH), F32),
        buf((n, tile, DH)), buf((n, tok, DH)), buf((n, tok, DH)),
        buf((n, g, tile, DH)), buf((n, g, tile, DH)),
        buf((n, tile, DH)), buf((n, tile, DH)), buf((n, DH, tile), F32),
        buf((n, 1, tile), F32), buf((n, tok, 1), jnp.int32),
        buf((ch, span)), buf((TAPS, ch, span)), buf((ch, span)),
        dma((3, n)), dma((3, n)), dma((n,)), dma((n,)), dma((m,)), dma((m,)),
        dma((m,)), dma((m,)), dma((n,)), dma((n,)), dma((n,)), dma((n,)),
        dma((2, n)), dma((2, n)), dma((2, g, n)), dma((2, g, n)), dma((2, g, n)), dma((2, g, n)), dma((3, 2)), dma((3, 2)),
    ]
    shapes = [(tok, colw), (tok, width), (tok, width), (tok, width), (ch, tok)]
    return tuple(pl.pallas_call(
        functools.partial(kernel, n, m, hc, g),
        out_shape=[jax.ShapeDtypeStruct(s, BF16) for s in shapes],
        in_specs=[vmem] * 10,
        out_specs=[vmem] * 5,
        scratch_shapes=scratch,
        compiler_params=pltpu.CompilerParams(
            collective_id=0, has_side_effects=True, vmem_limit_bytes=56 * 2**20
        ),
    )(q, k, v, segq, segk, w, emg, taps, ew, do))


def solution(mesh):
    n, m = mesh.shape["ctx"], mesh.shape["head"]
    rows = P("ctx", "head")
    in_specs = (
        rows, rows, rows, P(), P("head", None), P(None, "ctx"), P(None, None, "ctx"), P(), rows,
    )
    out_specs = (rows, rows, rows, rows, P(None, "ctx"))
    return jax.shard_map(
        functools.partial(body, n, m), mesh=mesh, in_specs=in_specs, out_specs=out_specs,
        check_vma=False,
    )
```
